32 devices in a mesh: groups: 2 (over x), row: 16 (over z, y, core).
Axes of the slice: x: 2, y: 2, z: 4, core: 2. Of those that a mesh axis runs over, the one named last changes fastest.
Arguments:
- pair_rows: bfloat16 [256, 128, 128], P(('groups', 'row')), parts along dimension 0, may hold values from -6 to 6
- in_gain: float32 [128], replicated, may hold values from 0.1 to 1.9
- w_left: bfloat16 [128, 128], replicated, may hold values from -0.5 to 0.5
- w_left_gate: bfloat16 [128, 128], replicated, may hold values from -0.5 to 0.5
- w_right: bfloat16 [128, 128], replicated, may hold values from -0.5 to 0.5
- w_right_gate: bfloat16 [128, 128], replicated, may hold values from -0.5 to 0.5
- w_gate: bfloat16 [128, 128], replicated, may hold values from -0.5 to 0.5
- w_out: bfloat16 [128, 128], replicated, may hold values from -0.5 to 0.5
- out_gain: float32 [128], replicated, may hold values from 0.1 to 1.9
- valid_len: int32 [2], P('groups'), parts along dimension 0, may hold values from 64 to 128
- window: int32 [2], P('groups'), parts along dimension 0, may hold values from 0 to 7
Outputs:
- update: bfloat16 [256, 16, 128], P(('groups', 'row')), parts along dimension 0
The draws below stay inside these ranges and needn't reach their ends.
There are 2 independent parts, one for each index of `groups`. The reference program is written for one: setup_inputs(seed, part) draws one part's arguments, and reference() takes and returns one part's arrays. A program takes and returns all parts, laid end to end along the dimension named above; an argument that names none is the same for every part. Nothing has to cross between parts.
All inputs are finite; a program needn't handle non-finite values.
Results may differ from the reference program's by a relative error of at most 0.0078.
Values may be sent and summed in bfloat16 or wider, within the bound.
No kernel may reach another device: no remote copies, remote signals or barrier semaphores. Data moves between devices by JAX's collectives and lax.ppermute only.
A program may use at most 128 MiB of HBM per device.

```python
import jax
import jax.numpy as jnp
from jax import lax

C = 128
TOKENS = 128


def steps_of(key, shape, shards, smallest, high):
    loudness, own = 1.0, jax.random.fold_in(key, 6)
    for axis_at, shards_of in shards:
        heights = jnp.exp(jax.random.uniform(jax.random.fold_in(own, axis_at), (shards_of,), jnp.float32, smallest / len(shards), high / len(shards)))
        loudness = loudness * jnp.repeat(heights, shape[axis_at] // shards_of).reshape([-1 if axis == axis_at else 1 for axis in range(len(shape))])
    return loudness


def scatter_about(own_key, shape, deviation, most, shards=(), kind=jnp.bfloat16):
    drawn = jax.random.normal(own_key, shape, jnp.float32) * deviation
    if len(shards) > 0:
        drawn = steps_of(own_key, shape, shards, -0.22, 0.18) * drawn
    return jnp.clip(drawn, min=-most, max=most).astype(kind)


def setup_inputs(seed: int = 0, part: int = 0) -> dict:
    seeds = jax.random.split(jax.random.key(seed), 12)
    part_splits = jax.random.split(jax.random.fold_in(seeds[11], part), 12)
    return {
        "pair_rows": scatter_about(part_splits[0], (TOKENS, TOKENS, C), 1.0, 6.0, ((0, 16),)),
        "in_gain": jnp.clip(1.0 + 0.18 * jax.random.normal(seeds[1], (C,), jnp.float32), 0.1, 1.9),
        "w_left": scatter_about(seeds[2], (C, C), C ** -0.5, 0.5),
        "w_left_gate": scatter_about(seeds[3], (C, C), C ** -0.5, 0.5),
        "w_right": scatter_about(seeds[4], (C, C), C ** -0.5, 0.5),
        "w_right_gate": scatter_about(seeds[5], (C, C), C ** -0.5, 0.5),
        "w_gate": scatter_about(seeds[6], (C, C), C ** -0.5, 0.5),
        "w_out": scatter_about(seeds[7], (C, C), C ** -0.5, 0.5),
        "out_gain": jnp.clip(1.0 + 0.18 * jax.random.normal(seeds[8], (C,), jnp.float32), 0.1, 1.9),
        "valid_len": jax.random.randint(part_splits[9], (1,), TOKENS // 2, TOKENS + 1).astype(jnp.int32),
        "window": jax.random.randint(part_splits[10], (1,), 0, 8).astype(jnp.int32),
    }


def layer_norm(values, gain):
    mean_v = lax.optimization_barrier(jnp.mean(values, axis=-1, keepdims=True))
    centered = values - mean_v
    variance_v = lax.optimization_barrier(jnp.mean(centered * centered, axis=-1, keepdims=True))
    return centered * lax.rsqrt(variance_v + 1e-05) * gain

def edge_of(normed_rows, w_value, w_gating, mask_rows):
    channels = normed_rows.shape[-1]
    flat_rows = normed_rows.reshape(-1, channels)
    value_part = jnp.dot(flat_rows, w_value, preferred_element_type=jnp.float32)
    gating = jnp.dot(flat_rows, w_gating, preferred_element_type=jnp.float32)
    return ((jax.nn.sigmoid(gating) * value_part).reshape(normed_rows.shape) * mask_rows).astype(jnp.bfloat16)

def reference(pair_rows, in_gain, w_left, w_left_gate, w_right, w_right_gate, w_gate, w_out, out_gain, valid_len, window):
    tokens_all = pair_rows.shape[0]
    channels = pair_rows.shape[2]
    width_win = tokens_all // 8
    normed = layer_norm(pair_rows.astype(jnp.float32), in_gain).astype(jnp.bfloat16)
    col_live = (jnp.arange(tokens_all, dtype=jnp.int32) < valid_len[0]).astype(jnp.float32)
    live_mask = (col_live[:, None] * col_live[None, :])[:, :, None]
    start_row = (window[0] * width_win).astype(jnp.int32)
    left_edge = edge_of(normed, w_left, w_left_gate, live_mask)
    win_rows = lax.dynamic_slice_in_dim(normed, start_row, width_win, 0)
    win_mask = lax.dynamic_slice_in_dim(live_mask, start_row, width_win, 0)
    right_edge = edge_of(win_rows, w_right, w_right_gate, win_mask)
    gate_in = lax.dynamic_slice_in_dim(normed, start_row, width_win, 1)
    gate_vals = jax.nn.sigmoid(jnp.dot(gate_in.reshape(-1, channels), w_gate, preferred_element_type=jnp.float32))
    gate_vals = gate_vals.reshape(tokens_all, width_win, channels)
    product = jnp.einsum('ikc,jkc->ijc', left_edge.astype(jnp.float32), right_edge.astype(jnp.float32))
    normed_out = layer_norm(product, out_gain).astype(jnp.bfloat16)
    projected = jnp.dot(normed_out.reshape(-1, channels), w_out, preferred_element_type=jnp.float32)
    return (gate_vals * projected.reshape(tokens_all, width_win, channels)).astype(jnp.bfloat16)
```

```python
import functools

import jax
import jax.numpy as jnp
from jax import lax
from jax.experimental import pallas as pl
from jax.experimental.pallas import tpu as pltpu
from jax.sharding import PartitionSpec as P

BLOCKS = 8
VMEM = pl.BlockSpec(memory_space=pltpu.VMEM)
SMEM = pl.BlockSpec(memory_space=pltpu.SMEM)


def sigmoid(values):
    return 0.5 * jnp.tanh(0.5 * values) + 0.5


def layer_norm(values, gain):
    scale = 1.0 / values.shape[-1]
    mean_v = jnp.sum(values, axis=-1, keepdims=True) * scale
    centered = values - mean_v
    variance_v = jnp.sum(centered * centered, axis=-1, keepdims=True) * scale
    return centered * lax.rsqrt(variance_v + 1e-05) * gain


def dot(left, right):
    return jnp.dot(left, right, preferred_element_type=jnp.float32)


def edge_chunk(x, gain, w, w_gating, live):
    normed = layer_norm(x.astype(jnp.float32), gain).astype(jnp.bfloat16)
    value = dot(normed, w)
    gating = dot(normed, w_gating)
    return normed, (sigmoid(gating) * value * live).astype(jnp.bfloat16)


def steps(count, body):
    if count <= 16:
        for step in range(count):
            body(step)
    else:
        pl.loop(0, count)(body)


def edge_body(chunk, scalars, x_ref, gain_ref, w_ref, wg_ref, out_ref):
    rows, tokens, _ = x_ref.shape
    per_row = tokens // chunk
    gain = gain_ref[...]
    valid, first = scalars[0], scalars[1]
    ids = lax.broadcasted_iota(jnp.int32, (chunk, 1), 0)

    def body(step):
        row, col = step // per_row, (step % per_row) * chunk
        here = jnp.logical_and(first + row < valid, ids + col < valid)
        _, edge = edge_chunk(
            x_ref[row, pl.ds(col, chunk), :], gain, w_ref[...], wg_ref[...], here.astype(jnp.float32)
        )
        out_ref[row, pl.ds(col, chunk), :] = edge.astype(out_ref.dtype)

    steps(rows * per_row, body)


def left_body(chunk, scalars, x_ref, gain_ref, w_ref, wg_ref, wo_ref, out_ref, gate_ref):
    edge_body(chunk, scalars, x_ref, gain_ref, w_ref, wg_ref, out_ref)
    rows, width, channels = gate_ref.shape
    start = pl.multiple_of(scalars[2], width)
    gain = gain_ref[...]

    def body(row):
        x = x_ref[row, pl.ds(start, width), :]
        normed = layer_norm(x.astype(jnp.float32), gain).astype(jnp.bfloat16)
        gate_ref[row] = sigmoid(dot(normed, wo_ref[...]))

    steps(rows, body)


def finish_body(pieces, left_ref, gate_ref, w_out_ref, gain_ref, *refs):
    right_refs, out_ref, product = refs[:pieces], refs[-2], refs[-1]
    rows, tokens, channels = left_ref.shape
    base = 0
    for right_ref in right_refs:
        height = right_ref.shape[0]

        def body(j, right_ref=right_ref, base=base):
            def over(k, acc):
                at = pl.ds(k * 128, 128)
                r = right_ref[j, at, :].astype(jnp.float32).reshape(-1, 8, channels)
                return tuple(
                    acc[i]
                    + jnp.sum(left_ref[i, at, :].astype(jnp.float32).reshape(-1, 8, channels) * r, axis=0)
                    for i in range(rows)
                )

            acc = tuple(jnp.zeros((8, channels), jnp.float32) for _ in range(rows))
            if tokens == 128:
                acc = over(0, acc)
            else:
                acc = lax.fori_loop(0, tokens // 128, over, acc)
            for i in range(rows):
                product[i, pl.ds(base + j, 1), :] = jnp.sum(acc[i], axis=0, keepdims=True)

        steps(height, body)
        base += height
    gain = gain_ref[...]
    flat = product[...].reshape(rows * base, channels)
    normed = layer_norm(flat, gain).astype(jnp.bfloat16)
    result = dot(normed, w_out_ref[...]).reshape(rows, base, channels)
    out_ref[...] = (gate_ref[...] * result).astype(jnp.bfloat16)


def local(body, out_shape, n_in, scratch=(), smem=True):
    return pl.pallas_call(
        body,
        out_shape=out_shape,
        in_specs=([SMEM] if smem else []) + [VMEM] * (n_in - int(smem)),
        out_specs=jax.tree.map(lambda _: VMEM, out_shape),
        scratch_shapes=list(scratch),
        compiler_params=pltpu.CompilerParams(vmem_limit_bytes=60 * 2**20),
    )


def on_device(
    pair_rows, in_gain, w_left, w_left_gate, w_right, w_right_gate, w_gate, w_out, out_gain, valid_len, window, devices
):
    rows, tokens, channels = pair_rows.shape
    width = tokens // BLOCKS
    parts = width // rows
    half = rows // 2
    chunk = min(tokens, 128)
    me = lax.axis_index("row").astype(jnp.int32)
    block, part = me // parts, me % parts
    sub = block % 2
    valid, start = valid_len[0], window[0] * width
    differs = block ^ window[0]
    in_gain = in_gain.reshape(1, channels)
    out_gain = out_gain.reshape(1, channels)
    bf16, f32 = jnp.bfloat16, jnp.float32

    def swap(values, mask):
        return lax.ppermute(values, "row", [(i, i ^ mask) for i in range(devices)])

    halves = pair_rows.reshape(2, half, tokens, channels)
    sent = lax.dynamic_index_in_dim(halves, 1 - sub, 0, keepdims=False)
    kept = lax.dynamic_index_in_dim(halves, sub, 0, keepdims=False)
    piece = jnp.where(differs & 1 == 0, kept, swap(sent, parts))

    left, gate = local(
        functools.partial(left_body, chunk),
        (
            jax.ShapeDtypeStruct((rows, tokens, channels), bf16),
            jax.ShapeDtypeStruct((rows, width, channels), f32),
        ),
        6,
    )(jnp.stack([valid, me * rows, start]), pair_rows, in_gain, w_left, w_left_gate, w_gate)

    bit = 2
    while bit < BLOCKS:
        piece = jnp.where(differs & bit == 0, piece, swap(piece, parts * bit))
        bit *= 2

    first = start + part * rows + sub * half
    right = local(
        functools.partial(edge_body, chunk), jax.ShapeDtypeStruct((half, tokens, channels), bf16), 5
    )(jnp.stack([valid, first, start]), piece, in_gain, w_right, w_right_gate)

    held = [right, swap(right, parts)]
    order = [(0, 0), (0, 1)]
    bit = 1
    while bit < parts:
        held = held + [swap(values, bit) for values in held]
        order = order + [(p ^ bit, s) for p, s in order]
        bit *= 2

    def to_slots(values):
        values = jnp.where(sub == 0, values, values[:, :, ::-1])
        bit = 1
        while bit < parts:
            view = values.reshape(rows, parts // (2 * bit), 2, bit, 2, half, channels)
            values = jnp.where(part & bit == 0, view, view[:, :, ::-1]).reshape(values.shape)
            bit *= 2
        return values

    gate_slots = to_slots(gate.reshape(rows, parts, 2, half, channels)).reshape(rows, width, channels)
    out = local(
        functools.partial(finish_body, len(held)),
        jax.ShapeDtypeStruct((rows, width, channels), bf16),
        4 + len(held),
        [pltpu.VMEM((rows, width, channels), f32)],
        smem=False,
    )(left, gate_slots, w_out, out_gain, *held)
    return to_slots(out.reshape(rows, parts, 2, half, channels)).reshape(rows, width, channels)


def solution(mesh):
    return jax.shard_map(
        functools.partial(on_device, devices=mesh.shape["row"]),
        mesh=mesh,
        in_specs=(P(("groups", "row"), None, None),) + (P(),) * 8 + (P("groups"),) * 2,
        out_specs=P(("groups", "row"), None, None),
        check_vma=False,
    )
```

```python
import functools

import jax
import jax.numpy as jnp
from jax import lax
from jax.experimental import pallas as pl
from jax.experimental.pallas import tpu as pltpu
from jax.sharding import PartitionSpec as P

BLOCKS = 8
QUAD = 4
GROUPS = ((0, 1, 2, 3), (4, 5, 6, 7))
VMEM = pl.BlockSpec(memory_space=pltpu.VMEM)


def sigmoid(values):
    return 0.5 * jnp.tanh(0.5 * values) + 0.5


def layer_norm(values, gain):
    scale = 1.0 / values.shape[-1]
    mean_v = jnp.sum(values, axis=-1, keepdims=True) * scale
    centered = values - mean_v
    variance_v = jnp.sum(centered * centered, axis=-1, keepdims=True) * scale
    return centered * lax.rsqrt(variance_v + 1e-05) * gain


def dot(left, right):
    return jnp.dot(left, right, preferred_element_type=jnp.float32)


def scalar(ref, slot):
    return ref[0:1, slot : slot + 1][0, 0]


def steps(count, body):
    if count <= 16:
        for step in range(count):
            body(step)
    else:
        pl.loop(0, count)(body)


def edge_rows(chunk, first, valid, read, gain_ref, w_ref, wg_ref, out_ref):
    rows, tokens, _ = out_ref.shape
    per_row = tokens // chunk
    gain = gain_ref[...]
    ids = lax.broadcasted_iota(jnp.int32, (chunk, 1), 0)

    def body(step):
        row, col = step // per_row, (step % per_row) * chunk
        here = jnp.logical_and(first + row < valid, ids + col < valid)
        normed = layer_norm(read(row, pl.ds(col, chunk)).astype(jnp.float32), gain).astype(jnp.bfloat16)
        edge = sigmoid(dot(normed, wg_ref[...])) * dot(normed, w_ref[...]) * here.astype(jnp.float32)
        out_ref[row, pl.ds(col, chunk), :] = edge.astype(jnp.bfloat16).astype(out_ref.dtype)

    steps(rows * per_row, body)


def left_body(chunk, scalars, x_ref, gain_ref, w_ref, wg_ref, wo_ref, out_ref, gate_ref):
    edge_rows(
        chunk, scalar(scalars, 1), scalar(scalars, 0), lambda row, at: x_ref[row, at, :], gain_ref, w_ref, wg_ref, out_ref
    )
    rows, width, channels = gate_ref.shape
    at = pl.ds(pl.multiple_of(scalar(scalars, 2), width), width)
    gain = gain_ref[...]

    def body(row):
        normed = layer_norm(x_ref[row, at, :].astype(jnp.float32), gain).astype(jnp.bfloat16)
        gate_ref[row] = sigmoid(dot(normed, wo_ref[...]))

    steps(rows, body)


def right_body(chunk, scalars, *refs):
    candidates, (gain_ref, w_ref, wg_ref, out_ref) = refs[:-4], refs[-4:]
    which = scalar(scalars, 4)

    def read(row, at):
        value = candidates[0][row, at, :]
        for d in range(1, len(candidates)):
            value = jnp.where(which == d, candidates[d][row, at, :], value)
        return value

    edge_rows(chunk, scalar(scalars, 3), scalar(scalars, 0), read, gain_ref, w_ref, wg_ref, out_ref)


def contract(places, small, which, part, left_ref, right_ref, lanes, store):
    rows, tokens, channels = left_ref.shape
    depth = min(tokens, 128)
    for at_piece, (p, d) in enumerate(places):
        base = (part ^ p) * rows + (which ^ d) * small

        def over(k, first, at_piece=at_piece):
            at = pl.ds(k * depth, depth)
            rights = [
                right_ref[at_piece * small + t, at, :].astype(jnp.float32).reshape(-1, 8, channels)
                for t in range(small)
            ]
            for i in range(rows):
                l = left_ref[i, at, :].reshape(-1, 8, channels)
                for t in range(small):
                    here = pl.ds((t * rows + i) * 8, 8)
                    total = jnp.sum(l * rights[t], axis=0)
                    lanes[here, :] = total if first else lanes[here, :] + total

        over(0, True)
        if tokens > depth:
            pl.loop(1, tokens // depth)(lambda k: over(k, False))
        for t in range(small):
            total = lanes[pl.ds(t * rows * 8, rows, stride=8), :]
            for s in range(1, 8):
                total = total + lanes[pl.ds(t * rows * 8 + s, rows, stride=8), :]
            store(base + t, at_piece * small + t, total)


def early_body(order, small, scalars, left_ref, *refs):
    right_refs, out_ref, lanes = refs[:-2], refs[-2], refs[-1]
    at_row = 0
    for right_ref, places in zip(right_refs, order):

        def store(j, held_at, total, at_row=at_row):
            out_ref[at_row + held_at] = total

        contract(places, small, scalar(scalars, 4), scalar(scalars, 5), left_ref, right_ref, lanes, store)
        at_row += right_ref.shape[0]


def finish_body(early_order, n_early, order, small, scalars, left_ref, gate_ref, w_out_ref, gain_ref, *refs):
    out_ref, product, result, lanes = refs[-4:]
    rows, tokens, channels = left_ref.shape
    width = out_ref.shape[1]
    which, part = scalar(scalars, 4), scalar(scalars, 5)
    right_refs = refs[:-4]
    early_rows = [ref.at[t] for ref in right_refs[:n_early] for t in range(ref.shape[0])]
    right_refs = right_refs[n_early:]
    for at_piece, (p, d) in enumerate(sum(early_order, [])):
        for t in range(small):
            product[(part ^ p) * rows + (which ^ d) * small + t] = early_rows[at_piece * small + t][...]

    def store(j, held_at, total):
        product[j] = total

    for right_ref, places in zip(right_refs, order):
        contract(places, small, which, part, left_ref, right_ref, lanes, store)
    normed = layer_norm(product[...].reshape(width * rows, channels), gain_ref[...]).astype(jnp.bfloat16)
    result[...] = dot(normed, w_out_ref[...])
    for i in range(rows):
        out_ref[i] = (gate_ref[i] * result[pl.ds(i, width, stride=rows), :]).astype(jnp.bfloat16)


def prepare_body(rows, width, gain_ref, later_ref, valid_ref, window_ref, gain_out, later_out, numbers_ref):
    gain_out[...] = gain_ref[...]
    later_out[...] = later_ref[...]
    small, parts = rows // QUAD, width // rows
    me = lax.axis_index("row").astype(jnp.int32)
    block, part = lax.div(me, parts), lax.rem(me, parts)
    window = window_ref[...]
    which = (window ^ block) & (QUAD - 1)
    start = window * width
    at = lax.broadcasted_iota(jnp.int32, numbers_ref.shape, 1)
    values = [valid_ref[...], me * rows, start, start + part * rows + which * small, which, part]
    numbers = jnp.zeros(numbers_ref.shape, jnp.int32)
    for slot, value in enumerate(values):
        numbers = jnp.where(at == slot, value, numbers)
    numbers_ref[...] = numbers


def size(values):
    return values.size * values.dtype.itemsize


def local(body, out_shape, scalars, *operands, scratch=()):
    outs = jax.tree.leaves(out_shape)
    need = sum(size(v) for v in operands) + sum(size(v) for v in outs)
    return pl.pallas_call(
        body,
        out_shape=out_shape,
        in_specs=[VMEM] * (1 + len(operands)),
        out_specs=jax.tree.map(lambda _: VMEM, out_shape),
        scratch_shapes=list(scratch),
        compiler_params=pltpu.CompilerParams(vmem_limit_bytes=min(60 * 2**20, 2 * need + 8 * 2**20)),
    )(scalars, *operands)


def on_device(
    pair_rows, in_gain, w_left, w_left_gate, w_right, w_right_gate, w_gate, w_out, out_gain, valid_len, window, devices
):
    rows, tokens, channels = pair_rows.shape
    width = tokens // BLOCKS
    parts = width // rows
    small = rows // QUAD
    chunk = min(tokens, 128)
    bf16, f32 = jnp.bfloat16, jnp.float32
    differs = lax.div(lax.axis_index("row").astype(jnp.int32), parts) ^ window[0]
    gain_shape = jax.ShapeDtypeStruct((1, channels), f32)
    in_gain, out_gain, scalars = pl.pallas_call(
        functools.partial(prepare_body, rows, width),
        out_shape=(gain_shape, gain_shape, jax.ShapeDtypeStruct((1, 128), jnp.int32)),
        in_specs=[VMEM] * 4,
        out_specs=(VMEM,) * 3,
        compiler_params=pltpu.CompilerParams(vmem_limit_bytes=8 * 2**20),
    )(in_gain.reshape(1, channels), out_gain.reshape(1, channels), valid_len.reshape(1, 1), window.reshape(1, 1))

    def swap(values, mask):
        return lax.ppermute(values, "row", [(i, i ^ mask) for i in range(devices)])

    got = {d: swap(pair_rows[d * small : (d + 1) * small], parts * d) for d in reversed(range(1, QUAD))}
    right = local(
        functools.partial(right_body, chunk),
        jax.ShapeDtypeStruct((small, tokens, channels), bf16),
        scalars, pair_rows[:small], *[got[d] for d in range(1, QUAD)], in_gain, w_right, w_right_gate,
    )
    left, gate = local(
        functools.partial(left_body, chunk),
        (
            jax.ShapeDtypeStruct((rows, tokens, channels), f32),
            jax.ShapeDtypeStruct((rows, width, channels), f32),
        ),
        scalars, pair_rows, in_gain, w_left, w_left_gate, w_gate,
    )
    bit = QUAD
    while bit < BLOCKS:
        other, left = lax.optimization_barrier((swap(right, parts * bit), left))
        right = jnp.where(differs & bit == 0, right, other)
        bit *= 2

    held, order = [right], [[(0, 0)]]
    for d in reversed(range(1, QUAD)):
        held.append(swap(right, parts * d))
        order.append([(0, d)])
    bit = 1
    while bit < parts:
        if bit > 1:
            held, order = [jnp.concatenate(held)], [sum(order, [])]
        held = held + [swap(values, bit) for values in held]
        order = order + [[(p ^ bit, d) for p, d in places] for places in order]
        bit *= 2

    lanes = pltpu.VMEM((small * rows * 8, channels), f32)
    groups = GROUPS if len(held) == 8 else (range(len(held)),)
    early, early_order = [], []
    for group in groups[:-1]:
        chosen = [order[i] for i in group]
        early_order += chosen
        early.append(
            local(
                functools.partial(early_body, chosen, small),
                jax.ShapeDtypeStruct((sum(held[i].shape[0] for i in group), rows, channels), f32),
                scalars, left, *[held[i] for i in group],
                scratch=[lanes],
            )
        )
    late_order = [order[i] for i in groups[-1]]
    late = [held[i] for i in groups[-1]]
    return local(
        functools.partial(finish_body, early_order, len(early), late_order, small),
        jax.ShapeDtypeStruct((rows, width, channels), bf16),
        scalars, left, gate, w_out, out_gain, *early, *late,
        scratch=[pltpu.VMEM((width, rows, channels), f32), pltpu.VMEM((width * rows, channels), f32), lanes],
    )


def solution(mesh):
    return jax.shard_map(
        functools.partial(on_device, devices=mesh.shape["row"]),
        mesh=mesh,
        in_specs=(P(("groups", "row"), None, None),) + (P(),) * 8 + (P("groups"),) * 2,
        out_specs=P(("groups", "row"), None, None),
        check_vma=False,
    )
```

```python
import functools

import jax
import jax.numpy as jnp
from jax import lax
from jax.experimental import pallas as pl
from jax.experimental.pallas import tpu as pltpu
from jax.sharding import PartitionSpec as P

BLOCKS = 8
QUAD = 4
FIRST = (3, 2, 1)
SECOND = (3, 1, 2)
GROUPS = ((0, 1, 2, 3, 4, 5), (6, 7))
VMEM = pl.BlockSpec(memory_space=pltpu.VMEM)


def sigmoid(values):
    return 0.5 * jnp.tanh(0.5 * values) + 0.5


def layer_norm(values, gain):
    scale = 1.0 / values.shape[-1]
    mean_v = jnp.sum(values, axis=-1, keepdims=True) * scale
    centered = values - mean_v
    variance_v = jnp.sum(centered * centered, axis=-1, keepdims=True) * scale
    return centered * lax.rsqrt(variance_v + 1e-05) * gain


def dot(left, right):
    return jnp.dot(left, right, preferred_element_type=jnp.float32)


def scalar(ref, slot):
    return ref[0:1, slot : slot + 1][0, 0]


def steps(count, body):
    if count <= 16:
        for step in range(count):
            body(step)
    else:
        pl.loop(0, count)(body)


def edge_rows(chunk, first, valid, read, gain_ref, w_ref, wg_ref, out_ref):
    rows, tokens, _ = out_ref.shape
    per_row = tokens // chunk
    gain = gain_ref[...]
    ids = lax.broadcasted_iota(jnp.int32, (chunk, 1), 0)

    def body(step):
        row, col = step // per_row, (step % per_row) * chunk
        here = jnp.logical_and(first + row < valid, ids + col < valid)
        normed = layer_norm(read(row, pl.ds(col, chunk)).astype(jnp.float32), gain).astype(jnp.bfloat16)
        edge = sigmoid(dot(normed, wg_ref[...])) * dot(normed, w_ref[...]) * here.astype(jnp.float32)
        out_ref[row, pl.ds(col, chunk), :] = edge.astype(jnp.bfloat16).astype(out_ref.dtype)

    steps(rows * per_row, body)


def left_body(chunk, scalars, x_ref, gain_ref, w_ref, wg_ref, wo_ref, out_ref, gate_ref):
    edge_rows(
        chunk, scalar(scalars, 1), scalar(scalars, 0), lambda row, at: x_ref[row, at, :], gain_ref, w_ref, wg_ref, out_ref
    )
    rows, width, channels = gate_ref.shape
    at = pl.ds(pl.multiple_of(scalar(scalars, 2), width), width)
    gain = gain_ref[...]

    def body(row):
        normed = layer_norm(x_ref[row, at, :].astype(jnp.float32), gain).astype(jnp.bfloat16)
        gate_ref[row] = sigmoid(dot(normed, wo_ref[...]))

    steps(rows, body)


def right_body(chunk, scalars, *refs):
    candidates, (gain_ref, w_ref, wg_ref, out_ref) = refs[:-4], refs[-4:]
    which = scalar(scalars, 4)

    def read(row, at):
        value = candidates[0][row, at, :]
        for d in range(1, len(candidates)):
            value = jnp.where(which == d, candidates[d][row, at, :], value)
        return value

    edge_rows(chunk, scalar(scalars, 3), scalar(scalars, 0), read, gain_ref, w_ref, wg_ref, out_ref)


def contract(places, small, which, part, left_ref, right_ref, lanes, store):
    rows, tokens, channels = left_ref.shape
    depth = min(tokens, 128)
    for at_piece, (p, d) in enumerate(places):
        base = (part ^ p) * rows + (which ^ d) * small

        def over(k, first, at_piece=at_piece):
            at = pl.ds(k * depth, depth)
            rights = [
                right_ref[at_piece * small + t, at, :].astype(jnp.float32).reshape(-1, 8, channels)
                for t in range(small)
            ]
            for i in range(rows):
                l = left_ref[i, at, :].reshape(-1, 8, channels)
                for t in range(small):
                    here = pl.ds((t * rows + i) * 8, 8)
                    total = jnp.sum(l * rights[t], axis=0)
                    lanes[here, :] = total if first else lanes[here, :] + total

        over(0, True)
        if tokens > depth:
            pl.loop(1, tokens // depth)(lambda k: over(k, False))
        for t in range(small):
            total = lanes[pl.ds(t * rows * 8, rows, stride=8), :]
            for s in range(1, 8):
                total = total + lanes[pl.ds(t * rows * 8 + s, rows, stride=8), :]
            store(base + t, at_piece * small + t, total)


def early_body(order, small, scalars, left_ref, *refs):
    right_refs, out_ref, lanes = refs[:-2], refs[-2], refs[-1]
    at_row = 0
    for right_ref, places in zip(right_refs, order):

        def store(j, held_at, total, at_row=at_row):
            out_ref[at_row + held_at] = total

        contract(places, small, scalar(scalars, 4), scalar(scalars, 5), left_ref, right_ref, lanes, store)
        at_row += right_ref.shape[0]


def finish_body(early_order, n_early, order, small, scalars, left_ref, gate_ref, w_out_ref, gain_ref, *refs):
    out_ref, product, result, lanes = refs[-4:]
    rows, tokens, channels = left_ref.shape
    width = out_ref.shape[1]
    which, part = scalar(scalars, 4), scalar(scalars, 5)
    right_refs = refs[:-4]
    early_rows = [ref.at[t] for ref in right_refs[:n_early] for t in range(ref.shape[0])]
    right_refs = right_refs[n_early:]
    for at_piece, (p, d) in enumerate(sum(early_order, [])):
        for t in range(small):
            product[(part ^ p) * rows + (which ^ d) * small + t] = early_rows[at_piece * small + t][...]

    def store(j, held_at, total):
        product[j] = total

    for right_ref, places in zip(right_refs, order):
        contract(places, small, which, part, left_ref, right_ref, lanes, store)
    normed = layer_norm(product[...].reshape(width * rows, channels), gain_ref[...]).astype(jnp.bfloat16)
    result[...] = dot(normed, w_out_ref[...])
    for i in range(rows):
        out_ref[i] = (gate_ref[i] * result[pl.ds(i, width, stride=rows), :]).astype(jnp.bfloat16)


def prepare_body(rows, width, gain_ref, later_ref, valid_ref, window_ref, gain_out, later_out, numbers_ref):
    gain_out[...] = gain_ref[...]
    later_out[...] = later_ref[...]
    small, parts = rows // QUAD, width // rows
    me = lax.axis_index("row").astype(jnp.int32)
    block, part = lax.div(me, parts), lax.rem(me, parts)
    window = window_ref[...]
    which = (window ^ block) & (QUAD - 1)
    start = window * width
    at = lax.broadcasted_iota(jnp.int32, numbers_ref.shape, 1)
    values = [valid_ref[...], me * rows, start, start + part * rows + which * small, which, part]
    numbers = jnp.zeros(numbers_ref.shape, jnp.int32)
    for slot, value in enumerate(values):
        numbers = jnp.where(at == slot, value, numbers)
    numbers_ref[...] = numbers


def size(values):
    return values.size * values.dtype.itemsize


def local(body, out_shape, scalars, *operands, scratch=()):
    outs = jax.tree.leaves(out_shape)
    need = sum(size(v) for v in operands) + sum(size(v) for v in outs)
    return pl.pallas_call(
        body,
        out_shape=out_shape,
        in_specs=[VMEM] * (1 + len(operands)),
        out_specs=jax.tree.map(lambda _: VMEM, out_shape),
        scratch_shapes=list(scratch),
        compiler_params=pltpu.CompilerParams(vmem_limit_bytes=min(60 * 2**20, 2 * need + 8 * 2**20)),
    )(scalars, *operands)


def on_device(
    pair_rows, in_gain, w_left, w_left_gate, w_right, w_right_gate, w_gate, w_out, out_gain, valid_len, window, devices
):
    rows, tokens, channels = pair_rows.shape
    width = tokens // BLOCKS
    parts = width // rows
    small = rows // QUAD
    chunk = min(tokens, 128)
    bf16, f32 = jnp.bfloat16, jnp.float32
    differs = lax.div(lax.axis_index("row").astype(jnp.int32), parts) ^ window[0]
    gain_shape = jax.ShapeDtypeStruct((1, channels), f32)
    in_gain, out_gain, scalars = pl.pallas_call(
        functools.partial(prepare_body, rows, width),
        out_shape=(gain_shape, gain_shape, jax.ShapeDtypeStruct((1, 128), jnp.int32)),
        in_specs=[VMEM] * 4,
        out_specs=(VMEM,) * 3,
        compiler_params=pltpu.CompilerParams(vmem_limit_bytes=8 * 2**20),
    )(in_gain.reshape(1, channels), out_gain.reshape(1, channels), valid_len.reshape(1, 1), window.reshape(1, 1))

    def swap(values, mask):
        return lax.ppermute(values, "row", [(i, i ^ mask) for i in range(devices)])

    got = {d: swap(pair_rows[d * small : (d + 1) * small], parts * d) for d in FIRST}
    right = local(
        functools.partial(right_body, chunk),
        jax.ShapeDtypeStruct((small, tokens, channels), bf16),
        scalars, pair_rows, *[got[d] for d in range(1, QUAD)], in_gain, w_right, w_right_gate,
    )
    left, gate = local(
        functools.partial(left_body, chunk),
        (
            jax.ShapeDtypeStruct((rows, tokens, channels), f32),
            jax.ShapeDtypeStruct((rows, width, channels), f32),
        ),
        scalars, pair_rows, in_gain, w_left, w_left_gate, w_gate,
    )
    bit = QUAD
    while bit < BLOCKS:
        other, left = lax.optimization_barrier((swap(right, parts * bit), left))
        right = jnp.where(differs & bit == 0, right, other)
        bit *= 2

    held, order = [right], [[(0, 0)]]
    for d in SECOND:
        held.append(swap(right, parts * d))
        order.append([(0, d)])
    bit = 1
    while bit < parts:
        if bit > 1:
            held, order = [jnp.concatenate(held)], [sum(order, [])]
        held = held + [swap(values, bit) for values in held]
        order = order + [[(p ^ bit, d) for p, d in places] for places in order]
        bit *= 2

    lanes = pltpu.VMEM((small * rows * 8, channels), f32)
    groups = GROUPS if len(held) == 8 else (range(len(held)),)
    early, early_order = [], []
    for group in groups[:-1]:
        chosen = [order[i] for i in group]
        early_order += chosen
        early.append(
            local(
                functools.partial(early_body, chosen, small),
                jax.ShapeDtypeStruct((sum(held[i].shape[0] for i in group), rows, channels), f32),
                scalars, left, *[held[i] for i in group],
                scratch=[lanes],
            )
        )
    late_order = [order[i] for i in groups[-1]]
    late = [held[i] for i in groups[-1]]
    return local(
        functools.partial(finish_body, early_order, len(early), late_order, small),
        jax.ShapeDtypeStruct((rows, width, channels), bf16),
        scalars, left, gate, w_out, out_gain, *early, *late,
        scratch=[pltpu.VMEM((width, rows, channels), f32), pltpu.VMEM((width * rows, channels), f32), lanes],
    )


def solution(mesh):
    return jax.shard_map(
        functools.partial(on_device, devices=mesh.shape["row"]),
        mesh=mesh,
        in_specs=(P(("groups", "row"), None, None),) + (P(),) * 8 + (P("groups"),) * 2,
        out_specs=P(("groups", "row"), None, None),
        check_vma=False,
    )
```

```python
import functools

import jax
import jax.numpy as jnp
from jax import lax
from jax.experimental import pallas as pl
from jax.experimental.pallas import tpu as pltpu
from jax.sharding import PartitionSpec as P

BLOCKS = 8
QUAD = 4
CHUNK = 256
FIRST = (3, 2, 1)
SECOND = (3, 1, 2)
GROUPS = ((0, 1, 2, 3, 4), (5, 6, 7))
VMEM = pl.BlockSpec(memory_space=pltpu.VMEM)


def sigmoid(values):
    return 0.5 * jnp.tanh(0.5 * values) + 0.5


def layer_norm(values, gain):
    scale = 1.0 / values.shape[-1]
    mean_v = jnp.sum(values, axis=-1, keepdims=True) * scale
    centered = values - mean_v
    variance_v = jnp.sum(centered * centered, axis=-1, keepdims=True) * scale
    return centered * lax.rsqrt(variance_v + 1e-05) * gain


def dot(left, right):
    return jnp.dot(left, right, preferred_element_type=jnp.float32)


def scalar(ref, slot):
    return ref[0:1, slot : slot + 1][0, 0]


def steps(count, body):
    if count <= 16:
        for step in range(count):
            body(step)
    else:
        pl.loop(0, count)(body)


def edge_rows(chunk, first, valid, read, gain_ref, w_ref, wg_ref, out_ref):
    rows, tokens, channels = out_ref.shape
    deep = min(tokens, chunk)
    high = min(max(chunk // tokens, 1), rows)
    per_row = tokens // deep
    gain = gain_ref[...]
    joined = jnp.concatenate([wg_ref[...], w_ref[...]], axis=1)
    ids = [lax.broadcasted_iota(jnp.int32, (high, deep, 1), axis) for axis in (0, 1)]

    def body(step):
        row, col = step // per_row * high, (step % per_row) * deep
        here = jnp.logical_and(ids[0] + (first + row) < valid, ids[1] + col < valid)
        values = read(pl.ds(row, high), pl.ds(col, deep)).astype(jnp.float32).reshape(high * deep, channels)
        both = dot(layer_norm(values, gain).astype(jnp.bfloat16), joined)
        edge = (sigmoid(both[:, :channels]) * both[:, channels:]).reshape(high, deep, channels)
        edge = (edge * here.astype(jnp.float32)).astype(jnp.bfloat16)
        out_ref[pl.ds(row, high), pl.ds(col, deep), :] = edge.astype(out_ref.dtype)

    steps(rows // high * per_row, body)


def left_body(chunk, scalars, x_ref, gain_ref, w_ref, wg_ref, wo_ref, out_ref, gate_ref):
    edge_rows(
        chunk, scalar(scalars, 1), scalar(scalars, 0), lambda row, at: x_ref[row, at, :], gain_ref, w_ref, wg_ref, out_ref
    )
    rows, width, channels = gate_ref.shape
    at = pl.ds(pl.multiple_of(scalar(scalars, 2), width), width)
    gain = gain_ref[...]

    def body(row):
        normed = layer_norm(x_ref[row, at, :].astype(jnp.float32), gain).astype(jnp.bfloat16)
        gate_ref[row] = sigmoid(dot(normed, wo_ref[...]))

    steps(rows, body)


def right_body(chunk, scalars, *refs):
    candidates, (gain_ref, w_ref, wg_ref, out_ref) = refs[:-4], refs[-4:]
    which = scalars[0:1, 4:5].reshape(1, 1, 1)

    def read(row, at):
        value = candidates[0][row, at, :].astype(jnp.float32)
        for d in range(1, len(candidates)):
            value = jnp.where(which == d, candidates[d][row, at, :].astype(jnp.float32), value)
        return value

    edge_rows(chunk, scalar(scalars, 3), scalar(scalars, 0), read, gain_ref, w_ref, wg_ref, out_ref)


def contract(places, small, which, part, left_ref, right_ref, lanes, store):
    rows, tokens, channels = left_ref.shape
    depth = min(tokens, 128)
    for at_piece, (p, d) in enumerate(places):
        base = (part ^ p) * rows + (which ^ d) * small

        def over(k, first, at_piece=at_piece):
            at = pl.ds(k * depth, depth)
            rights = [
                right_ref[at_piece * small + t, at, :].astype(jnp.float32).reshape(-1, 8, channels)
                for t in range(small)
            ]
            for i in range(rows):
                l = left_ref[i, at, :].reshape(-1, 8, channels)
                for t in range(small):
                    here = pl.ds((t * rows + i) * 8, 8)
                    total = jnp.sum(l * rights[t], axis=0)
                    lanes[here, :] = total if first else lanes[here, :] + total

        over(0, True)
        if tokens > depth:
            pl.loop(1, tokens // depth)(lambda k: over(k, False))
        for t in range(small):
            total = lanes[pl.ds(t * rows * 8, rows, stride=8), :]
            for s in range(1, 8):
                total = total + lanes[pl.ds(t * rows * 8 + s, rows, stride=8), :]
            store(base + t, at_piece * small + t, total)


def project(product, w_out_ref, gain_ref):
    normed = layer_norm(product, gain_ref[...]).astype(jnp.bfloat16)
    return dot(normed, w_out_ref[...])


def early_body(order, small, scalars, left_ref, w_out_ref, gain_ref, *refs):
    right_refs, out_ref, product, lanes = refs[:-3], refs[-3], refs[-2], refs[-1]
    at_row = 0
    for right_ref, places in zip(right_refs, order):

        def store(j, held_at, total, at_row=at_row):
            product[at_row + held_at] = total

        contract(places, small, scalar(scalars, 4), scalar(scalars, 5), left_ref, right_ref, lanes, store)
        at_row += right_ref.shape[0]
    out_ref[...] = project(product[...].reshape(-1, product.shape[-1]), w_out_ref, gain_ref).reshape(out_ref.shape)


def finish_body(early_order, n_early, order, small, scalars, left_ref, gate_ref, w_out_ref, gain_ref, *refs):
    out_ref, product, result, lanes = refs[-4:]
    rows, tokens, channels = left_ref.shape
    width = out_ref.shape[1]
    which, part = scalar(scalars, 4), scalar(scalars, 5)
    early_refs, right_refs = refs[:n_early], refs[n_early:-4]

    def row_of(place, t):
        return ((part ^ place[0]) * rows + (which ^ place[1]) * small + t) * rows

    at_row = 0
    for right_ref, places in zip(right_refs, order):

        def store(j, held_at, total, at_row=at_row):
            product[at_row + held_at] = total

        contract(places, small, which, part, left_ref, right_ref, lanes, store)
        at_row += right_ref.shape[0]
    late = project(product[...].reshape(-1, channels), w_out_ref, gain_ref)
    for at_piece, place in enumerate(sum(order, [])):
        for t in range(small):
            at = (at_piece * small + t) * rows
            result[pl.ds(row_of(place, t), rows), :] = late[at : at + rows]
    early_rows = [ref.at[t] for ref in early_refs for t in range(ref.shape[0])]
    for at_piece, place in enumerate(sum(early_order, [])):
        for t in range(small):
            result[pl.ds(row_of(place, t), rows), :] = early_rows[at_piece * small + t][...]
    for i in range(rows):
        out_ref[i] = (gate_ref[i] * result[pl.ds(i, width, stride=rows), :]).astype(jnp.bfloat16)


def prepare_body(rows, width, gain_ref, later_ref, valid_ref, window_ref, gain_out, later_out, numbers_ref):
    gain_out[...] = gain_ref[...]
    later_out[...] = later_ref[...]
    small, parts = rows // QUAD, width // rows
    me = lax.axis_index("row").astype(jnp.int32)
    block, part = lax.div(me, parts), lax.rem(me, parts)
    window = window_ref[...]
    which = (window ^ block) & (QUAD - 1)
    start = window * width
    at = lax.broadcasted_iota(jnp.int32, numbers_ref.shape, 1)
    values = [valid_ref[...], me * rows, start, start + part * rows + which * small, which, part]
    numbers = jnp.zeros(numbers_ref.shape, jnp.int32)
    for slot, value in enumerate(values):
        numbers = jnp.where(at == slot, value, numbers)
    numbers_ref[...] = numbers


def size(values):
    return values.size * values.dtype.itemsize


def local(body, out_shape, scalars, *operands, scratch=()):
    outs = jax.tree.leaves(out_shape)
    need = sum(size(v) for v in operands) + sum(size(v) for v in outs)
    return pl.pallas_call(
        body,
        out_shape=out_shape,
        in_specs=[VMEM] * (1 + len(operands)),
        out_specs=jax.tree.map(lambda _: VMEM, out_shape),
        scratch_shapes=list(scratch),
        compiler_params=pltpu.CompilerParams(vmem_limit_bytes=min(60 * 2**20, 2 * need + 8 * 2**20)),
    )(scalars, *operands)


def on_device(
    pair_rows, in_gain, w_left, w_left_gate, w_right, w_right_gate, w_gate, w_out, out_gain, valid_len, window, devices
):
    rows, tokens, channels = pair_rows.shape
    width = tokens // BLOCKS
    parts = width // rows
    small = rows // QUAD
    chunk = CHUNK
    bf16, f32 = jnp.bfloat16, jnp.float32
    differs = lax.div(lax.axis_index("row").astype(jnp.int32), parts) ^ window[0]
    gain_shape = jax.ShapeDtypeStruct((1, channels), f32)
    in_gain, out_gain, scalars = pl.pallas_call(
        functools.partial(prepare_body, rows, width),
        out_shape=(gain_shape, gain_shape, jax.ShapeDtypeStruct((1, 128), jnp.int32)),
        in_specs=[VMEM] * 4,
        out_specs=(VMEM,) * 3,
        compiler_params=pltpu.CompilerParams(vmem_limit_bytes=8 * 2**20),
    )(in_gain.reshape(1, channels), out_gain.reshape(1, channels), valid_len.reshape(1, 1), window.reshape(1, 1))

    def swap(values, mask):
        return lax.ppermute(values, "row", [(i, i ^ mask) for i in range(devices)])

    got = {d: swap(pair_rows[d * small : (d + 1) * small], parts * d) for d in FIRST}
    right = local(
        functools.partial(right_body, chunk),
        jax.ShapeDtypeStruct((small, tokens, channels), bf16),
        scalars, pair_rows, *[got[d] for d in range(1, QUAD)], in_gain, w_right, w_right_gate,
    )
    left, gate = local(
        functools.partial(left_body, chunk),
        (
            jax.ShapeDtypeStruct((rows, tokens, channels), f32),
            jax.ShapeDtypeStruct((rows, width, channels), f32),
        ),
        scalars, pair_rows, in_gain, w_left, w_left_gate, w_gate,
    )
    bit = QUAD
    while bit < BLOCKS:
        other, left = lax.optimization_barrier((swap(right, parts * bit), left))
        right = jnp.where(differs & bit == 0, right, other)
        bit *= 2

    held, order = [right], [[(0, 0)]]
    for d in SECOND:
        held.append(swap(right, parts * d))
        order.append([(0, d)])
    bit = 1
    while bit < parts:
        if bit > 1:
            held, order = [jnp.concatenate(held)], [sum(order, [])]
        held = held + [swap(values, bit) for values in held]
        order = order + [[(p ^ bit, d) for p, d in places] for places in order]
        bit *= 2

    lanes = pltpu.VMEM(((small * rows + 1) * 8, channels), f32)
    groups = GROUPS if len(held) == 8 else (range(len(held)),)
    early, early_order = [], []
    for group in groups[:-1]:
        chosen = [order[i] for i in group]
        early_order += chosen
        early.append(
            local(
                functools.partial(early_body, chosen, small),
                jax.ShapeDtypeStruct((sum(held[i].shape[0] for i in group), rows, channels), f32),
                scalars, left, w_out, out_gain, *[held[i] for i in group],
                scratch=[pltpu.VMEM((sum(held[i].shape[0] for i in group), rows, channels), f32), lanes],
            )
        )
    late_order = [order[i] for i in groups[-1]]
    late = [held[i] for i in groups[-1]]
    return local(
        functools.partial(finish_body, early_order, len(early), late_order, small),
        jax.ShapeDtypeStruct((rows, width, channels), bf16),
        scalars, left, gate, w_out, out_gain, *early, *late,
        scratch=[
            pltpu.VMEM((sum(h.shape[0] for h in late), rows, channels), f32),
            pltpu.VMEM(((width + 1) * rows, channels), f32),
            lanes,
        ],
    )


def solution(mesh):
    return jax.shard_map(
        functools.partial(on_device, devices=mesh.shape["row"]),
        mesh=mesh,
        in_specs=(P(("groups", "row"), None, None),) + (P(),) * 8 + (P("groups"),) * 2,
        out_specs=P(("groups", "row"), None, None),
        check_vma=False,
    )
```

```python
import functools

import jax
import jax.numpy as jnp
from jax import lax
from jax.experimental import pallas as pl
from jax.experimental.pallas import tpu as pltpu
from jax.sharding import PartitionSpec as P

BLOCKS = 8
QUAD = 4
SLOTS = 6
CHUNK = 256
FIRST = (3, 2, 1)
SECOND = (3, 1, 2)
GROUPS = ((0, 1, 2, 3, 4), (5, 6, 7))
VMEM = pl.BlockSpec(memory_space=pltpu.VMEM)


def sigmoid(values):
    return 0.5 * jnp.tanh(0.5 * values) + 0.5


def layer_norm(values, gain):
    scale = 1.0 / values.shape[-1]
    mean_v = jnp.sum(values, axis=-1, keepdims=True) * scale
    centered = values - mean_v
    variance_v = jnp.sum(centered * centered, axis=-1, keepdims=True) * scale
    return centered * lax.rsqrt(variance_v + 1e-05) * gain


def dot(left, right):
    return jnp.dot(left, right, preferred_element_type=jnp.float32)


def scalar(ref, slot):
    return ref[0:1, slot : slot + 1][0, 0]


def steps(count, body):
    if count <= 16:
        for step in range(count):
            body(step)
    else:
        pl.loop(0, count)(body)


def edge_rows(chunk, first, valid, read, gain_ref, w_ref, wg_ref, out_ref):
    rows, tokens, channels = out_ref.shape
    deep = min(tokens, chunk)
    high = min(max(chunk // tokens, 1), rows)
    per_row = tokens // deep
    gain = gain_ref[...]
    joined = jnp.concatenate([wg_ref[...], w_ref[...]], axis=1)
    ids = [lax.broadcasted_iota(jnp.int32, (high, deep, 1), axis) for axis in (0, 1)]

    def body(step):
        row, col = step // per_row * high, (step % per_row) * deep
        here = jnp.logical_and(ids[0] + (first + row) < valid, ids[1] + col < valid)
        values = read(pl.ds(row, high), pl.ds(col, deep)).astype(jnp.float32).reshape(high * deep, channels)
        both = dot(layer_norm(values, gain).astype(jnp.bfloat16), joined)
        edge = (sigmoid(both[:, :channels]) * both[:, channels:]).reshape(high, deep, channels)
        edge = (edge * here.astype(jnp.float32)).astype(jnp.bfloat16)
        out_ref[pl.ds(row, high), pl.ds(col, deep), :] = edge.astype(out_ref.dtype)

    steps(rows // high * per_row, body)


def left_body(chunk, scalars, x_ref, gain_ref, w_ref, wg_ref, wo_ref, out_ref, gate_ref):
    edge_rows(
        chunk, scalar(scalars, 1), scalar(scalars, 0), lambda row, at: x_ref[row, at, :], gain_ref, w_ref, wg_ref, out_ref
    )
    rows, width, channels = gate_ref.shape
    at = pl.ds(pl.multiple_of(scalar(scalars, 2), width), width)
    gain = gain_ref[...]

    def body(row):
        normed = layer_norm(x_ref[row, at, :].astype(jnp.float32), gain).astype(jnp.bfloat16)
        gate_ref[row] = sigmoid(dot(normed, wo_ref[...]))

    steps(rows, body)


def right_body(chunk, scalars, *refs):
    candidates, (gain_ref, w_ref, wg_ref, out_ref) = refs[:-4], refs[-4:]
    which = scalars[0:1, 4:5].reshape(1, 1, 1)

    def read(row, at):
        value = candidates[0][row, at, :].astype(jnp.float32)
        for d in range(1, len(candidates)):
            value = jnp.where(which == d, candidates[d][row, at, :].astype(jnp.float32), value)
        return value

    edge_rows(chunk, scalar(scalars, 3), scalar(scalars, 0), read, gain_ref, w_ref, wg_ref, out_ref)


def contract(places, small, which, part, left_ref, right_ref, lanes, slot, store):
    rows, tokens, channels = left_ref.shape
    depth = min(tokens, 128)
    for at_piece, (p, d) in enumerate(places):
        base = (part ^ p) * rows + (which ^ d) * small
        skip = (slot + at_piece) % SLOTS * (small * rows + 1) * 8

        def over(k, first, at_piece=at_piece, skip=skip):
            at = pl.ds(k * depth, depth)
            rights = [
                right_ref[at_piece * small + t, at, :].astype(jnp.float32).reshape(-1, 8, channels)
                for t in range(small)
            ]
            for i in range(rows):
                l = left_ref[i, at, :].reshape(-1, 8, channels)
                for t in range(small):
                    here = pl.ds(skip + (t * rows + i) * 8, 8)
                    total = jnp.sum(l * rights[t], axis=0)
                    lanes[here, :] = total if first else lanes[here, :] + total

        over(0, True)
        if tokens > depth:
            pl.loop(1, tokens // depth)(lambda k: over(k, False))
        for t in range(small):
            total = lanes[pl.ds(skip + t * rows * 8, rows, stride=8), :]
            for s in range(1, 8):
                total = total + lanes[pl.ds(skip + t * rows * 8 + s, rows, stride=8), :]
            store(base + t, at_piece * small + t, total)


def project(product, w_out_ref, gain_ref):
    normed = layer_norm(product, gain_ref[...]).astype(jnp.bfloat16)
    return dot(normed, w_out_ref[...])


def early_body(order, small, scalars, left_ref, w_out_ref, gain_ref, *refs):
    right_refs, out_ref, product, lanes = refs[:-3], refs[-3], refs[-2], refs[-1]
    at_row = 0
    for right_ref, places in zip(right_refs, order):

        def store(j, held_at, total, at_row=at_row):
            product[at_row + held_at] = total

        contract(places, small, scalar(scalars, 4), scalar(scalars, 5), left_ref, right_ref, lanes, at_row // small, store)
        at_row += right_ref.shape[0]
    out_ref[...] = project(product[...].reshape(-1, product.shape[-1]), w_out_ref, gain_ref).reshape(out_ref.shape)


def finish_body(early_order, n_early, order, small, scalars, left_ref, gate_ref, w_out_ref, gain_ref, *refs):
    out_ref, product, result, lanes = refs[-4:]
    rows, tokens, channels = left_ref.shape
    width = out_ref.shape[1]
    which, part = scalar(scalars, 4), scalar(scalars, 5)
    early_refs, right_refs = refs[:n_early], refs[n_early:-4]

    def row_of(place, t):
        return ((part ^ place[0]) * rows + (which ^ place[1]) * small + t) * rows

    at_row = 0
    for right_ref, places in zip(right_refs, order):

        def store(j, held_at, total, at_row=at_row):
            product[at_row + held_at] = total

        contract(places, small, which, part, left_ref, right_ref, lanes, at_row // small, store)
        at_row += right_ref.shape[0]
    late = project(product[...].reshape(-1, channels), w_out_ref, gain_ref)
    for at_piece, place in enumerate(sum(order, [])):
        for t in range(small):
            at = (at_piece * small + t) * rows
            result[pl.ds(row_of(place, t), rows), :] = late[at : at + rows]
    early_rows = [ref.at[t] for ref in early_refs for t in range(ref.shape[0])]
    for at_piece, place in enumerate(sum(early_order, [])):
        for t in range(small):
            result[pl.ds(row_of(place, t), rows), :] = early_rows[at_piece * small + t][...]
    for i in range(rows):
        out_ref[i] = (gate_ref[i] * result[pl.ds(i, width, stride=rows), :]).astype(jnp.bfloat16)


def prepare_body(rows, width, gain_ref, later_ref, valid_ref, window_ref, gain_out, later_out, numbers_ref):
    gain_out[...] = gain_ref[...]
    later_out[...] = later_ref[...]
    small, parts = rows // QUAD, width // rows
    me = lax.axis_index("row").astype(jnp.int32)
    block, part = lax.div(me, parts), lax.rem(me, parts)
    window = window_ref[...]
    which = (window ^ block) & (QUAD - 1)
    start = window * width
    at = lax.broadcasted_iota(jnp.int32, numbers_ref.shape, 1)
    values = [valid_ref[...], me * rows, start, start + part * rows + which * small, which, part]
    numbers = jnp.zeros(numbers_ref.shape, jnp.int32)
    for slot, value in enumerate(values):
        numbers = jnp.where(at == slot, value, numbers)
    numbers_ref[...] = numbers


def size(values):
    return values.size * values.dtype.itemsize


def local(body, out_shape, scalars, *operands, scratch=()):
    outs = jax.tree.leaves(out_shape)
    need = sum(size(v) for v in operands) + sum(size(v) for v in outs)
    return pl.pallas_call(
        body,
        out_shape=out_shape,
        in_specs=[VMEM] * (1 + len(operands)),
        out_specs=jax.tree.map(lambda _: VMEM, out_shape),
        scratch_shapes=list(scratch),
        compiler_params=pltpu.CompilerParams(vmem_limit_bytes=min(60 * 2**20, 2 * need + 8 * 2**20)),
    )(scalars, *operands)


def on_device(
    pair_rows, in_gain, w_left, w_left_gate, w_right, w_right_gate, w_gate, w_out, out_gain, valid_len, window, devices
):
    rows, tokens, channels = pair_rows.shape
    width = tokens // BLOCKS
    parts = width // rows
    small = rows // QUAD
    chunk = CHUNK
    bf16, f32 = jnp.bfloat16, jnp.float32
    differs = lax.div(lax.axis_index("row").astype(jnp.int32), parts) ^ window[0]
    gain_shape = jax.ShapeDtypeStruct((1, channels), f32)
    in_gain, out_gain, scalars = pl.pallas_call(
        functools.partial(prepare_body, rows, width),
        out_shape=(gain_shape, gain_shape, jax.ShapeDtypeStruct((1, 128), jnp.int32)),
        in_specs=[VMEM] * 4,
        out_specs=(VMEM,) * 3,
        compiler_params=pltpu.CompilerParams(vmem_limit_bytes=8 * 2**20),
    )(in_gain.reshape(1, channels), out_gain.reshape(1, channels), valid_len.reshape(1, 1), window.reshape(1, 1))

    def swap(values, mask):
        return lax.ppermute(values, "row", [(i, i ^ mask) for i in range(devices)])

    got = {d: swap(pair_rows[d * small : (d + 1) * small], parts * d) for d in FIRST}
    right = local(
        functools.partial(right_body, chunk),
        jax.ShapeDtypeStruct((small, tokens, channels), bf16),
        scalars, pair_rows, *[got[d] for d in range(1, QUAD)], in_gain, w_right, w_right_gate,
    )
    left, gate = local(
        functools.partial(left_body, chunk),
        (
            jax.ShapeDtypeStruct((rows, tokens, channels), f32),
            jax.ShapeDtypeStruct((rows, width, channels), f32),
        ),
        scalars, pair_rows, in_gain, w_left, w_left_gate, w_gate,
    )
    bit = QUAD
    while bit < BLOCKS:
        other, left = lax.optimization_barrier((swap(right, parts * bit), left))
        right = jnp.where(differs & bit == 0, right, other)
        bit *= 2

    held, order = [right], [[(0, 0)]]
    for d in SECOND:
        held.append(swap(right, parts * d))
        order.append([(0, d)])
    bit = 1
    while bit < parts:
        if bit > 1:
            held, order = [jnp.concatenate(held)], [sum(order, [])]
        held = held + [swap(values, bit) for values in held]
        order = order + [[(p ^ bit, d) for p, d in places] for places in order]
        bit *= 2

    lanes = pltpu.VMEM((SLOTS * (small * rows + 1) * 8, channels), f32)
    groups = GROUPS if len(held) == 8 else (range(len(held)),)
    early, early_order = [], []
    for group in groups[:-1]:
        chosen = [order[i] for i in group]
        early_order += chosen
        early.append(
            local(
                functools.partial(early_body, chosen, small),
                jax.ShapeDtypeStruct((sum(held[i].shape[0] for i in group), rows, channels), f32),
                scalars, left, w_out, out_gain, *[held[i] for i in group],
                scratch=[pltpu.VMEM((sum(held[i].shape[0] for i in group), rows, channels), f32), lanes],
            )
        )
    late_order = [order[i] for i in groups[-1]]
    late = [held[i] for i in groups[-1]]
    return local(
        functools.partial(finish_body, early_order, len(early), late_order, small),
        jax.ShapeDtypeStruct((rows, width, channels), bf16),
        scalars, left, gate, w_out, out_gain, *early, *late,
        scratch=[
            pltpu.VMEM((sum(h.shape[0] for h in late), rows, channels), f32),
            pltpu.VMEM(((width + 1) * rows, channels), f32),
            lanes,
        ],
    )


def solution(mesh):
    return jax.shard_map(
        functools.partial(on_device, devices=mesh.shape["row"]),
        mesh=mesh,
        in_specs=(P(("groups", "row"), None, None),) + (P(),) * 8 + (P("groups"),) * 2,
        out_specs=P(("groups", "row"), None, None),
        check_vma=False,
    )
```
